32 devices in a mesh: lev: 2 (over x), gx: 4 (over z), gy: 4 (over y, core).
Axes of the slice: x: 2, y: 2, z: 4, core: 2. Of those that a mesh axis runs over, the one named last changes fastest.
Arguments:
- initial_conc: float32 [4, 4, 256, 512], P(None, 'lev', 'gx', 'gy'), may hold values from -6 to 6
- diffusivity: float32 [4, 256, 512], P('lev', 'gx', 'gy'), may hold values from 0.02 to 0.2
- wind_east: float32 [4, 256, 512], P('lev', 'gx', 'gy'), may hold values from -0.4 to 0.4
- wind_north: float32 [4, 256, 512], P('lev', 'gx', 'gy'), may hold values from -0.4 to 0.4
- level_weight: float32 [4, 4], P(None, 'lev'), may hold values from 0.05 to 0.5
- sounding_owner: int32 [8192, 1], P(('gx', 'gy')), may hold values from 0 to 15; in each aligned block of 512 rows (0 to 511, 512 to 1023, ...) at most 64 rows name the same one
- sounding_column: int32 [8192], P(('gx', 'gy')), may hold values from 0 to 8191
- observed: float32 [8192], P(('gx', 'gy')), may hold values from -15 to 15
Outputs:
- forecast: float32 [4, 4, 256, 512], P(None, 'lev', 'gx', 'gy')
- model_column: float32 [8192], P(('gx', 'gy'))
- gradient: float32 [4, 4, 256, 512], P(None, 'lev', 'gx', 'gy')
The draws below stay inside these ranges and needn't reach their ends.
Inputs may be any that keep to these rules, and one draw needn't show every extreme that they name: `sounding_owner`: among the 512 soundings of one device, at most 64 have the same owner, and this many is reached.
All inputs are finite; a program needn't handle non-finite values.
Results may differ from the reference program's by a relative error of at most 0.00002.
Values sent between devices are 32-bit elements; how exact they have to be, the bound alone decides.
A program may use at most 64 MiB of HBM per device.

```python
import math
import jax
import jax.numpy as jnp
import numpy as np

TRACERS = 4
STEPS = 4
CX = 64
CY = 128
SND_DEV = 512
CAP = 64
LEVELS = 4
NX = 256
NY = 512
SOUNDINGS = 8192
N_GX = 4
N_GY = 4


def set_ends(entries, own_key, low, top_value):
    longest = entries.shape.index(max(entries.shape))
    spots = []
    for shift in (0, 1):
        where = [jax.random.randint(jax.random.fold_in(own_key, axis), (), 0, length) for axis, length in enumerate(entries.shape)]
        where[longest] = (where[longest] + shift) % entries.shape[longest]
        spots.append(tuple(where))
    return entries.at[spots[0]].set(low).at[spots[1]].set(top_value)


def level_of(key, extent, pieces, least, largest):
    def one(axis_at, shards_of):
        steps = jax.random.uniform(jax.random.fold_in(jax.random.fold_in(key, 6), axis_at), (shards_of,), jnp.float32, least / len(pieces), largest / len(pieces))
        return jnp.repeat(jnp.exp(steps), extent[axis_at] // shards_of).reshape((-1,) + (1,) * (len(extent) - axis_at - 1))

    gain = one(*pieces[0])
    for cut in pieces[1:]:
        gain = gain * one(*cut)
    return gain


def shared_out(stream_key, own, number, rows, amount, top, reach, slope):
    sequence = jax.random.permutation(stream_key, amount)
    heavy_load, common = portions_of(amount, rows * top, reach, slope, True), portions_of(amount, rows * top, reach, slope, False)
    places = jnp.arange(amount)

    def named(sizes, rotation):
        used = int((sizes > 0).sum())
        fixed = max(1, used // 4)
        passed = fixed + (places - fixed + rotation * (used - fixed)) % max(1, amount - fixed)
        return jnp.zeros((amount,), jnp.int32).at[sequence[jnp.where(places < fixed, places, passed)]].set(jnp.asarray(sizes, jnp.int32))

    sizes = jnp.where(number % 4 == 0, named(heavy_load, number // 4), named(common, number - number // 4 - 1))
    mixed = jax.random.permutation(jax.random.fold_in(own, 3), amount)
    source_of, sink = mixed[0:amount // 2 * 2:2], mixed[1:amount // 2 * 2:2]
    slack = jnp.minimum(sizes[source_of] - 1, reach - sizes[sink]) // 2
    slack = jnp.where((source_of == sequence[0]) | (sink == sequence[0]) | (sizes[sink] == 0), 0, jnp.maximum(slack, 0))
    passed = jax.random.randint(jax.random.fold_in(own, 4), (amount // 2,), 0, 1 << 20) % (slack + 1)
    sizes = sizes.at[source_of].add(-passed).at[sink].add(passed)
    items = jnp.searchsorted(jnp.cumsum(sizes), jnp.arange(rows * top), side="right").astype(jnp.int32)
    table = items.reshape(top, rows).T
    table = table[jax.random.permutation(jax.random.fold_in(own, 1), rows)]
    rotation = jax.random.randint(jax.random.fold_in(own, 2), (rows, 1), 0, top)
    return jnp.take_along_axis(table, (jnp.arange(top)[None, :] + rotation) % top, axis=1)


def portions_of(count, total, reach, slope, full):
    weights = [(1 << 20) // math.isqrt(standing ** slope) + 1 for standing in range(1, count + 1)]
    largest = reach if full else min(reach, max(-(-total // count), total * weights[0] // sum(weights)))
    least = 1 if total - largest >= count - 1 else 0
    holding, rest = [largest] + [least] * (count - 1), total - largest - least * (count - 1)
    while rest > 0:
        movable = [i for i in range(1, count) if holding[i] < largest] or [i for i in range(1, count) if holding[i] < reach]
        whole, left = sum([weights[i] for i in movable]), rest
        for i in movable:
            addition = min(reach - holding[i], max(1, left * weights[i] // whole), rest)
            holding[i] = holding[i] + addition
            rest = rest - addition
    return np.array(holding)


def centred(rng, extent, spread, bound, cuts=(), kind=jnp.bfloat16):
    drawn = jax.random.normal(rng, extent, jnp.float32) * spread
    if len(cuts) > 0:
        drawn = level_of(rng, extent, cuts, -0.22, 0.18) * drawn
    return jnp.clip(drawn, min=-bound, max=bound).astype(kind)


def setup_inputs(seed: int = 0) -> dict:
    arg_keys = jax.random.split(jax.random.key(seed), 9)
    initial_conc = centred(arg_keys[0], (TRACERS, LEVELS, NX, NY), 1.0, 6.0, ((1, 2), (2, 4), (3, 4)), jnp.float32)
    diffusivity = jnp.clip(jnp.exp(math.log(0.2) - 2.3025851 * jax.random.uniform(arg_keys[1], (LEVELS, NX, NY), jnp.float32) ** level_of(arg_keys[1], (LEVELS, NX, NY), ((0, 2), (1, 4), (2, 4)), -0.2, 0.2)), 0.02, 0.2)
    wind_east = jnp.clip(jax.random.uniform(arg_keys[2], (LEVELS, NX, NY), jnp.float32, -0.4, 0.4) * level_of(arg_keys[2], (LEVELS, NX, NY), ((0, 2), (1, 4), (2, 4)), -0.4, 0.0), -0.4, 0.4)
    wind_north = jnp.clip(jax.random.uniform(arg_keys[3], (LEVELS, NX, NY), jnp.float32, -0.4, 0.4) * level_of(arg_keys[3], (LEVELS, NX, NY), ((0, 2), (1, 4), (2, 4)), -0.4, 0.0), -0.4, 0.4)
    level_weight = jnp.clip(jnp.exp(math.log(0.5) - 2.3025851 * jax.random.uniform(arg_keys[4], (TRACERS, LEVELS), jnp.float32) ** level_of(arg_keys[4], (TRACERS, LEVELS), ((1, 2),), -0.2, 0.2)), 0.05, 0.5)
    sounding_owner_keys = jax.random.split(jax.random.fold_in(arg_keys[5], 1), SOUNDINGS // SND_DEV)
    sounding_owner_turns = jax.random.permutation(jax.random.fold_in(arg_keys[5], 3), SOUNDINGS // SND_DEV)
    sounding_owner = jax.vmap(lambda own, number: shared_out(jax.random.fold_in(arg_keys[5], 2), own, number, SND_DEV, N_GX * N_GY, 1, CAP, 2))(sounding_owner_keys, sounding_owner_turns).reshape((SOUNDINGS, 1))
    sounding_column = set_ends(jax.random.randint(arg_keys[6], (SOUNDINGS,), 0, CX * CY), jax.random.fold_in(arg_keys[6], 1), 0, (CX * CY) - 1).astype(jnp.int32)
    observed = centred(arg_keys[7], (SOUNDINGS,), 3.0, 15.0, ((0, 16),), jnp.float32)
    return dict(initial_conc=initial_conc, diffusivity=diffusivity, wind_east=wind_east, wind_north=wind_north, level_weight=level_weight, sounding_owner=sounding_owner, sounding_column=sounding_column, observed=observed)


def neighbours(field):
    padded = jnp.pad(field, ((0, 0), (0, 0), (1, 1), (1, 1)))
    east = padded[:, :, 2:, 1:-1]
    west = padded[:, :, :-2, 1:-1]
    north = padded[:, :, 1:-1, 2:]
    south = padded[:, :, 1:-1, :-2]
    return east, west, north, south


def forward_step(conc, diffusivity, wind_east, wind_north):
    east, west, north, south = neighbours(conc)
    return conc + diffusivity * (east + west + north + south - 4.0 * conc) - 0.5 * wind_east * (east - west) - 0.5 * wind_north * (north - south)


def adjoint_step(adj, diffusivity, wind_east, wind_north):
    diffused = diffusivity * adj
    pushed_east = wind_east * adj
    pushed_north = wind_north * adj
    k_east, k_west, k_north, k_south = neighbours(diffused)
    u_east, u_west, u_north, u_south = neighbours(pushed_east)
    v_east, v_west, v_north, v_south = neighbours(pushed_north)
    lap = k_east + k_west + k_north + k_south - 4.0 * diffused
    return adj + lap + 0.5 * (u_east - u_west) + 0.5 * (v_north - v_south)


def reference(initial_conc, diffusivity, wind_east, wind_north, level_weight, sounding_owner, sounding_column, observed):
    conc = initial_conc
    for step in range(STEPS):
        conc = forward_step(conc, diffusivity, wind_east, wind_north)
    column_field = jnp.sum(level_weight[:, :, None, None] * conc, axis=(0, 1))
    owner = sounding_owner[:, 0]
    xcell = (owner // N_GY) * CX + sounding_column // CY
    ycell = (owner % N_GY) * CY + sounding_column % CY
    model_column = column_field[xcell, ycell]
    misfit = model_column - observed
    forcing = jnp.zeros((NX, NY), jnp.float32).at[xcell, ycell].add(misfit)
    adj = level_weight[:, :, None, None] * forcing[None, None, :, :]
    for step in range(STEPS):
        adj = adjoint_step(adj, diffusivity, wind_east, wind_north)
    return conc, model_column, adj
```

```python
import functools
import jax
import jax.numpy as jnp
from jax import lax
from jax.experimental import pallas as pl
from jax.experimental.pallas import tpu as pltpu
from jax.sharding import PartitionSpec as P

STEPS = 4
H = 2 * STEPS
MESH = pl.DeviceIdType.MESH
SIDES = [(-1, 0), (1, 0), (0, -1), (0, 1), (-1, -1), (-1, 1), (1, -1), (1, 1)]


def pieces(value):
    high = value.astype(jnp.bfloat16).astype(jnp.float32)
    rest = value - high
    middle = rest.astype(jnp.bfloat16).astype(jnp.float32)
    return high, middle, rest - middle


def kernel(
    sizes,
    conc_ref, diff_ref, east_ref, north_ref, weight_ref, owner_ref, column_ref, observed_ref,
    forecast_ref, model_ref, grad_ref,
    ext, other, pack, from_left, from_right, coef, mine, snd, count, part, arrived, values, returned,
    halo_send, halo_recv, snd_send, snd_recv, part_send, part_recv, back_send, back_recv,
):
    n_gx, n_gy, tracers, levels, cx, cy = sizes
    groups = n_gx * n_gy
    fields = tracers * levels
    rows, lanes = cx + 2 * H, 2 * cy
    lev, gx, gy = lax.axis_index("lev"), lax.axis_index("gx"), lax.axis_index("gy")
    me = gx * n_gy + gy

    def group_id(d):
        target = lax.rem(me + d, groups)
        return (lev, target // n_gy, lax.rem(target, n_gy))

    ext[:, 0:H, 0:cy] = jnp.zeros((ext.shape[0], H, cy), jnp.float32)
    ext[:, H + cx : rows, 0:cy] = jnp.zeros((ext.shape[0], H, cy), jnp.float32)
    from_left[...] = jnp.zeros(from_left.shape, jnp.float32)
    from_right[...] = jnp.zeros(from_right.shape, jnp.float32)

    barrier = pltpu.get_barrier_semaphore()

    def greet(d, carry):
        pl.semaphore_signal(barrier, inc=1, device_id=group_id(d), device_id_type=MESH)
        return carry

    lax.fori_loop(1, groups, greet, 0)
    pl.semaphore_signal(barrier, inc=1, device_id=(1 - lev, gx, gy), device_id_type=MESH)

    lane = lax.broadcasted_iota(jnp.int32, (cx, cy), 1)
    per = cy // (2 * H)
    packed = [jnp.zeros((cx, cy), jnp.float32) for _ in range(pack.shape[0])]
    for f in range(ext.shape[0]):
        if f < fields:
            field = conc_ref[f]
        else:
            which, l = divmod(f - fields, levels)
            field = (diff_ref, east_ref, north_ref)[which][l]
        ext[f, H : H + cx, 0:cy] = field
        g, at = divmod(f, per)
        shift = 2 * H * at
        moved = pltpu.roll(field, shift, axis=1) if shift else field
        slot = lax.rem(lane + H, cy) // (2 * H)
        packed[g] = jnp.where(slot == at, moved, packed[g])
    for g in range(pack.shape[0]):
        pack[g] = packed[g]
    owner, column = owner_ref[...], column_ref[...]
    nrow = owner.shape[0]
    mine[0:nrow] = ((owner // n_gy) * cx + column // cy).astype(jnp.float32)
    mine[nrow : 2 * nrow] = (lax.rem(owner, n_gy) * cy + lax.rem(column, cy)).astype(jnp.float32)
    mine[2 * nrow : 3 * nrow] = observed_ref[...]
    snd[me] = mine[...]

    pl.semaphore_wait(barrier, groups)

    def inside(dx, dy):
        x, y = gx + dx, gy + dy
        return (x >= 0) & (x < n_gx) & (y >= 0) & (y < n_gy)

    def halo_copy(k):
        dx, dy = SIDES[k]
        start, length, to = {-1: (0, H, H + cx), 0: (0, cx, H), 1: (cx - H, H, 0)}[dx]
        if dy == 0:
            src = ext.at[:, pl.ds(H + start, length), pl.ds(0, cy)]
            dst = ext.at[:, pl.ds(to, length), pl.ds(0, cy)]
        else:
            src = pack.at[:, pl.ds(start, length), :]
            dst = (from_right if dy < 0 else from_left).at[:, pl.ds(to, length), :]
        return pltpu.make_async_remote_copy(
            src_ref=src, dst_ref=dst, send_sem=halo_send.at[k], recv_sem=halo_recv.at[k],
            device_id=(lev, gx + dx, gy + dy), device_id_type=MESH,
        )

    for k, (dx, dy) in enumerate(SIDES):
        pl.when(inside(dx, dy))(lambda k=k: halo_copy(k).start())

    def snd_copy(d):
        return pltpu.make_async_remote_copy(
            src_ref=mine, dst_ref=snd.at[me], send_sem=snd_send.at[d], recv_sem=snd_recv.at[d],
            device_id=group_id(d), device_id_type=MESH,
        )

    def loop_over(low, high, body):
        def step(i, carry):
            body(i)
            return carry

        lax.fori_loop(low, high, step, 0)

    loop_over(1, groups, lambda d: snd_copy(d).start())

    for k, (dx, dy) in enumerate(SIDES):
        pl.when(inside(-dx, -dy))(lambda k=k: halo_copy(k).wait_recv())

    wide = lax.broadcasted_iota(jnp.int32, (rows, cy), 1)
    for g in range(pack.shape[0]):
        both = jnp.where(lax.rem(wide, 2 * H) < H, from_right[g], from_left[g])
        for at in range(min(per, ext.shape[0] - g * per)):
            shift = 2 * H * at
            moved = pltpu.roll(both, cy - shift, axis=1) if shift else both
            ext[g * per + at, :, cy:lanes] = jnp.where((wide < H) | (wide >= cy - H), moved, 0.0)
    for l in range(levels):
        kappa = ext[fields + l]
        u = 0.5 * ext[fields + levels + l]
        v = 0.5 * ext[fields + 2 * levels + l]
        coef[l, 0] = 1.0 - 4.0 * kappa
        coef[l, 1] = kappa - u
        coef[l, 2] = kappa + u
        coef[l, 3] = kappa - v
        coef[l, 4] = kappa + v

    def stepped(c, l):
        return (
            coef[l, 0] * c
            + coef[l, 1] * pltpu.roll(c, rows - 1, axis=0)
            + coef[l, 2] * pltpu.roll(c, 1, axis=0)
            + coef[l, 3] * pltpu.roll(c, lanes - 1, axis=1)
            + coef[l, 4] * pltpu.roll(c, 1, axis=1)
        )

    for step in range(STEPS):
        source, target = (ext, other) if step % 2 == 0 else (other, ext)
        if step == 1:
            for k, (dx, dy) in enumerate(SIDES):
                pl.when(inside(dx, dy))(lambda k=k: halo_copy(k).wait_send())
        if step < STEPS - 1:
            def advance(t):
                for l in range(levels):
                    target[t * levels + l] = stepped(source[t * levels + l], l)

            loop_over(0, tracers, advance)
        else:
            part[...] = jnp.zeros(part.shape, jnp.float32)

            def finish(t):
                total = part[...]
                for l in range(levels):
                    result = stepped(source[t * levels + l], l)
                    forecast_ref[t * levels + l] = result[H : H + cx, 0:cy]
                    total = total + weight_ref[t, l] * result
                part[...] = total

            loop_over(0, tracers, finish)

    part_copy = pltpu.make_async_remote_copy(
        src_ref=part, dst_ref=arrived, send_sem=part_send, recv_sem=part_recv,
        device_id=(1 - lev, gx, gy), device_id_type=MESH,
    )
    part_copy.start()

    loop_over(1, groups, lambda d: snd_copy(d).wait_recv())
    loop_over(1, groups, lambda d: snd_copy(d).wait_send())
    at_once = 4
    x0 = (gx * cx).astype(jnp.float32)
    y0 = (gy * cy).astype(jnp.float32)

    def row_of(base, kind):
        return jnp.concatenate(
            [snd[base + b, kind * nrow + r : kind * nrow + r + 1, :] for b in range(at_once) for r in range(nrow)],
            axis=1,
        )

    span = at_once * nrow * snd.shape[2]
    compact = cy + 2 * H
    count[...] = jnp.zeros(count.shape, jnp.float32)

    def tally(i):
        base = i * at_once
        xs = row_of(base, 0) - (x0 - H)
        ys = row_of(base, 1) - (y0 - H)
        obs = row_of(base, 2)
        at_x = lax.broadcasted_iota(jnp.int32, (rows, span), 0).astype(jnp.float32) == xs
        at_y = lax.broadcasted_iota(jnp.int32, (compact, span), 0).astype(jnp.float32) == ys
        stack = [jnp.where(at_x, 1.0, 0.0)] + [jnp.where(at_x, piece, 0.0) for piece in pieces(obs)]
        left = jnp.concatenate([s.astype(jnp.bfloat16) for s in stack], axis=0)
        right = jnp.where(at_y, 1.0, 0.0).astype(jnp.bfloat16)
        count[:, 0:compact] += lax.dot_general(
            left, right, (((1,), (1,)), ((), ())), preferred_element_type=jnp.float32
        )

    loop_over(0, groups // at_once, tally)

    part_copy.wait()
    field = part[...] + arrived[...]
    number = pltpu.roll(count[0:rows], lanes - H, axis=1)
    total = pltpu.roll(
        count[rows : 2 * rows] + count[2 * rows : 3 * rows] + count[3 * rows : 4 * rows], lanes - H, axis=1
    )
    forcing = number * field - total

    centre = field[H : H + cx, 0:cy]
    stacked = jnp.concatenate(list(pieces(centre)) + [jnp.zeros_like(centre)], axis=0)
    turned = stacked.T.astype(jnp.bfloat16)

    def look_up(i):
        base = i * at_once
        xs = row_of(base, 0) - x0
        ys = row_of(base, 1) - y0
        at_x = lax.broadcasted_iota(jnp.int32, (cx, span), 0).astype(jnp.float32) == xs
        at_y = lax.broadcasted_iota(jnp.int32, (cy, span), 0).astype(jnp.float32) == ys
        pick = jnp.where(at_x, 1.0, 0.0).astype(jnp.bfloat16)
        picked = jnp.dot(
            turned, jnp.concatenate([pick] * 4, axis=0), preferred_element_type=jnp.float32
        )
        found = jnp.sum(jnp.where(at_y, picked, 0.0), axis=0, keepdims=True)
        width = snd.shape[2]
        for b in range(at_once):
            for r in range(nrow):
                k = b * nrow + r
                values[base + b, r : r + 1, :] = found[:, k * width : (k + 1) * width]

    loop_over(0, groups // at_once, look_up)

    def back_copy(d):
        return pltpu.make_async_remote_copy(
            src_ref=values.at[lax.rem(me + d, groups)], dst_ref=returned.at[d],
            send_sem=back_send.at[d], recv_sem=back_recv.at[d],
            device_id=group_id(d), device_id_type=MESH,
        )

    loop_over(1, groups, lambda d: back_copy(d).start())

    for l in range(levels):
        adj = forcing
        for step in range(STEPS):
            adj = (
                coef[l, 0] * adj
                + pltpu.roll(coef[l, 2] * adj, rows - 1, axis=0)
                + pltpu.roll(coef[l, 1] * adj, 1, axis=0)
                + pltpu.roll(coef[l, 4] * adj, lanes - 1, axis=1)
                + pltpu.roll(coef[l, 3] * adj, 1, axis=1)
            )
        inner = adj[H : H + cx, 0:cy]
        for t in range(tracers):
            grad_ref[t * levels + l] = weight_ref[t, l] * inner

    loop_over(1, groups, lambda d: back_copy(d).wait_recv())
    model = values[me]
    for d in range(1, groups):
        model = model + returned[d]
    model_ref[...] = model
    loop_over(1, groups, lambda d: back_copy(d).wait_send())


def shards(n_gx, n_gy, initial_conc, diffusivity, wind_east, wind_north, level_weight, owner, column, observed):
    tracers, levels, cx, cy = initial_conc.shape
    fields = tracers * levels
    total = fields + 3 * levels
    groups = n_gx * n_gy
    count = column.shape[0]
    width = min(128, count)
    nrow = count // width
    rows, lanes = cx + 2 * H, 2 * cy
    per = cy // (2 * H)
    packs = -(-total // per)
    f32 = jnp.float32
    vmem = pl.BlockSpec(memory_space=pltpu.VMEM)
    dma = pltpu.SemaphoreType.DMA
    conc, model, grad = pl.pallas_call(
        functools.partial(kernel, (n_gx, n_gy, tracers, levels, cx, cy)),
        out_shape=(
            jax.ShapeDtypeStruct((fields, cx, cy), f32),
            jax.ShapeDtypeStruct((nrow, width), f32),
            jax.ShapeDtypeStruct((fields, cx, cy), f32),
        ),
        in_specs=[vmem] * 4 + [pl.BlockSpec(memory_space=pltpu.SMEM)] + [vmem] * 3,
        out_specs=(vmem, vmem, vmem),
        scratch_shapes=[
            pltpu.VMEM((total, rows, lanes), f32),
            pltpu.VMEM((fields, rows, lanes), f32),
            pltpu.VMEM((packs, cx, cy), f32),
            pltpu.VMEM((packs, rows, cy), f32),
            pltpu.VMEM((packs, rows, cy), f32),
            pltpu.VMEM((levels, 5, rows, lanes), f32),
            pltpu.VMEM((3 * nrow, width), f32),
            pltpu.VMEM((groups, 3 * nrow, width), f32),
            pltpu.VMEM((4 * rows, lanes), f32),
            pltpu.VMEM((rows, lanes), f32),
            pltpu.VMEM((rows, lanes), f32),
            pltpu.VMEM((groups, nrow, width), f32),
            pltpu.VMEM((groups, nrow, width), f32),
            dma((len(SIDES),)), dma((len(SIDES),)),
            dma((groups,)), dma((groups,)),
            dma, dma,
            dma((groups,)), dma((groups,)),
        ],
        compiler_params=pltpu.CompilerParams(
            collective_id=0, has_side_effects=True, vmem_limit_bytes=48 * 1024 * 1024
        ),
        cost_estimate=pl.CostEstimate(flops=2 * 10**9, bytes_accessed=2 * 10**6, transcendentals=0),
    )(
        initial_conc.reshape(fields, cx, cy), diffusivity, wind_east, wind_north, level_weight,
        owner.reshape(nrow, width), column.reshape(nrow, width), observed.reshape(nrow, width),
    )
    shape = (tracers, levels, cx, cy)
    return conc.reshape(shape), model.reshape(count), grad.reshape(shape)


def solution(mesh):
    return jax.shard_map(
        functools.partial(shards, mesh.shape["gx"], mesh.shape["gy"]),
        mesh=mesh,
        in_specs=(
            P(None, "lev", "gx", "gy"),
            P("lev", "gx", "gy"),
            P("lev", "gx", "gy"),
            P("lev", "gx", "gy"),
            P(None, "lev"),
            P(("gx", "gy"), None),
            P(("gx", "gy")),
            P(("gx", "gy")),
        ),
        out_specs=(P(None, "lev", "gx", "gy"), P(("gx", "gy")), P(None, "lev", "gx", "gy")),
        check_vma=False,
    )
```

```python
import functools
import jax
import jax.numpy as jnp
from jax import lax
from jax.experimental import pallas as pl
from jax.experimental.pallas import tpu as pltpu
from jax.sharding import PartitionSpec as P

STEPS = 4
H = 2 * STEPS
MESH = pl.DeviceIdType.MESH
SIDES = [(-1, 0), (1, 0), (0, -1), (0, 1), (-1, -1), (-1, 1), (1, -1), (1, 1)]


def pieces(value):
    high = value.astype(jnp.bfloat16).astype(jnp.float32)
    rest = value - high
    middle = rest.astype(jnp.bfloat16).astype(jnp.float32)
    return high, middle, rest - middle


def kernel(
    sizes,
    conc_ref, diff_ref, east_ref, north_ref, weight_ref, owner_ref, column_ref, observed_ref,
    forecast_ref, model_ref, grad_ref,
    ext, other, pack, from_left, from_right, coef, mine, snd, count, part, arrived, values, returned,
    halo_send, halo_recv, snd_send, snd_recv, part_send, part_recv, back_send, back_recv,
    owner_in, column_in, observed_in, load_sem,
):
    n_gx, n_gy, tracers, levels, cx, cy = sizes
    groups = n_gx * n_gy
    fields = tracers * levels
    rows, lanes = cx + 2 * H, 2 * cy
    lev, gx, gy = lax.axis_index("lev"), lax.axis_index("gx"), lax.axis_index("gy")
    me = gx * n_gy + gy

    def group_id(d):
        target = lax.rem(me + d, groups)
        return (lev, target // n_gy, lax.rem(target, n_gy))

    loads = []
    begin = 0
    for ref in (conc_ref, diff_ref, east_ref, north_ref):
        place = ext.at[pl.ds(begin, ref.shape[0]), pl.ds(H, cx), pl.ds(0, cy)]
        loads.append(pltpu.make_async_copy(ref, place, load_sem.at[len(loads)]))
        begin += ref.shape[0]
    for ref, place in ((owner_ref, owner_in), (column_ref, column_in), (observed_ref, observed_in)):
        loads.append(pltpu.make_async_copy(ref, place, load_sem.at[len(loads)]))
    for load in loads:
        load.start()

    ext[:, 0:H, 0:cy] = jnp.zeros((ext.shape[0], H, cy), jnp.float32)
    ext[:, H + cx : rows, 0:cy] = jnp.zeros((ext.shape[0], H, cy), jnp.float32)
    from_left[...] = jnp.zeros(from_left.shape, jnp.float32)
    from_right[...] = jnp.zeros(from_right.shape, jnp.float32)

    barrier = pltpu.get_barrier_semaphore()

    def greet(d, carry):
        pl.semaphore_signal(barrier, inc=1, device_id=group_id(d), device_id_type=MESH)
        return carry

    lax.fori_loop(1, groups, greet, 0)
    pl.semaphore_signal(barrier, inc=1, device_id=(1 - lev, gx, gy), device_id_type=MESH)

    for load in loads:
        load.wait()

    lane = lax.broadcasted_iota(jnp.int32, (cx, cy), 1)
    per = cy // (2 * H)
    packed = [jnp.zeros((cx, cy), jnp.float32) for _ in range(pack.shape[0])]
    for f in range(ext.shape[0]):
        field = ext[f, H : H + cx, 0:cy]
        g, at = divmod(f, per)
        shift = 2 * H * at
        moved = pltpu.roll(field, shift, axis=1) if shift else field
        slot = lax.rem(lane + H, cy) // (2 * H)
        packed[g] = jnp.where(slot == at, moved, packed[g])
    for g in range(pack.shape[0]):
        pack[g] = packed[g]
    owner, column = owner_in[...], column_in[...]
    nrow = owner.shape[0]
    mine[0:nrow] = ((owner // n_gy) * cx + column // cy).astype(jnp.float32)
    mine[nrow : 2 * nrow] = (lax.rem(owner, n_gy) * cy + lax.rem(column, cy)).astype(jnp.float32)
    mine[2 * nrow : 3 * nrow] = observed_in[...]
    snd[me] = mine[...]

    pl.semaphore_wait(barrier, groups)

    def inside(dx, dy):
        x, y = gx + dx, gy + dy
        return (x >= 0) & (x < n_gx) & (y >= 0) & (y < n_gy)

    def halo_copy(k):
        dx, dy = SIDES[k]
        start, length, to = {-1: (0, H, H + cx), 0: (0, cx, H), 1: (cx - H, H, 0)}[dx]
        if dy == 0:
            src = ext.at[:, pl.ds(H + start, length), pl.ds(0, cy)]
            dst = ext.at[:, pl.ds(to, length), pl.ds(0, cy)]
        else:
            src = pack.at[:, pl.ds(start, length), :]
            dst = (from_right if dy < 0 else from_left).at[:, pl.ds(to, length), :]
        return pltpu.make_async_remote_copy(
            src_ref=src, dst_ref=dst, send_sem=halo_send.at[k], recv_sem=halo_recv.at[k],
            device_id=(lev, gx + dx, gy + dy), device_id_type=MESH,
        )

    for k, (dx, dy) in enumerate(SIDES):
        pl.when(inside(dx, dy))(lambda k=k: halo_copy(k).start())

    def snd_copy(d):
        return pltpu.make_async_remote_copy(
            src_ref=mine, dst_ref=snd.at[me], send_sem=snd_send.at[d], recv_sem=snd_recv.at[d],
            device_id=group_id(d), device_id_type=MESH,
        )

    def loop_over(low, high, body):
        def step(i, carry):
            body(i)
            return carry

        lax.fori_loop(low, high, step, 0)

    loop_over(1, groups, lambda d: snd_copy(d).start())

    for k, (dx, dy) in enumerate(SIDES):
        pl.when(inside(-dx, -dy))(lambda k=k: halo_copy(k).wait_recv())

    wide = lax.broadcasted_iota(jnp.int32, (rows, cy), 1)
    for g in range(pack.shape[0]):
        both = jnp.where(lax.rem(wide, 2 * H) < H, from_right[g], from_left[g])
        for at in range(min(per, ext.shape[0] - g * per)):
            shift = 2 * H * at
            moved = pltpu.roll(both, cy - shift, axis=1) if shift else both
            ext[g * per + at, :, cy:lanes] = jnp.where((wide < H) | (wide >= cy - H), moved, 0.0)
    for l in range(levels):
        kappa = ext[fields + l]
        u = 0.5 * ext[fields + levels + l]
        v = 0.5 * ext[fields + 2 * levels + l]
        coef[l, 0] = 1.0 - 4.0 * kappa
        coef[l, 1] = kappa - u
        coef[l, 2] = kappa + u
        coef[l, 3] = kappa - v
        coef[l, 4] = kappa + v

    def stepped(c, l):
        return (
            coef[l, 0] * c
            + coef[l, 1] * pltpu.roll(c, rows - 1, axis=0)
            + coef[l, 2] * pltpu.roll(c, 1, axis=0)
            + coef[l, 3] * pltpu.roll(c, lanes - 1, axis=1)
            + coef[l, 4] * pltpu.roll(c, 1, axis=1)
        )

    for step in range(STEPS):
        source, target = (ext, other) if step % 2 == 0 else (other, ext)
        if step == 1:
            for k, (dx, dy) in enumerate(SIDES):
                pl.when(inside(dx, dy))(lambda k=k: halo_copy(k).wait_send())
        if step < STEPS - 1:
            def advance(t):
                for l in range(levels):
                    target[t * levels + l] = stepped(source[t * levels + l], l)

            loop_over(0, tracers, advance)
        else:
            part[...] = jnp.zeros(part.shape, jnp.float32)

            def finish(t):
                total = part[...]
                for l in range(levels):
                    result = stepped(source[t * levels + l], l)
                    forecast_ref[t * levels + l] = result[H : H + cx, 0:cy]
                    total = total + weight_ref[t, l] * result
                part[...] = total

            loop_over(0, tracers, finish)

    part_copy = pltpu.make_async_remote_copy(
        src_ref=part, dst_ref=arrived, send_sem=part_send, recv_sem=part_recv,
        device_id=(1 - lev, gx, gy), device_id_type=MESH,
    )
    part_copy.start()

    loop_over(1, groups, lambda d: snd_copy(d).wait_recv())
    loop_over(1, groups, lambda d: snd_copy(d).wait_send())
    at_once = 4
    x0 = (gx * cx).astype(jnp.float32)
    y0 = (gy * cy).astype(jnp.float32)

    def row_of(base, kind):
        return jnp.concatenate(
            [snd[base + b, kind * nrow + r : kind * nrow + r + 1, :] for b in range(at_once) for r in range(nrow)],
            axis=1,
        )

    span = at_once * nrow * snd.shape[2]
    compact = cy + 2 * H
    count[...] = jnp.zeros(count.shape, jnp.float32)

    def tally(i):
        base = i * at_once
        xs = row_of(base, 0) - (x0 - H)
        ys = row_of(base, 1) - (y0 - H)
        obs = row_of(base, 2)
        at_x = lax.broadcasted_iota(jnp.int32, (rows, span), 0).astype(jnp.float32) == xs
        at_y = lax.broadcasted_iota(jnp.int32, (compact, span), 0).astype(jnp.float32) == ys
        stack = [jnp.where(at_x, 1.0, 0.0)] + [jnp.where(at_x, piece, 0.0) for piece in pieces(obs)]
        left = jnp.concatenate([s.astype(jnp.bfloat16) for s in stack], axis=0)
        right = jnp.where(at_y, 1.0, 0.0).astype(jnp.bfloat16)
        count[:, 0:compact] += lax.dot_general(
            left, right, (((1,), (1,)), ((), ())), preferred_element_type=jnp.float32
        )

    loop_over(0, groups // at_once, tally)

    part_copy.wait()
    field = part[...] + arrived[...]
    number = pltpu.roll(count[0:rows], lanes - H, axis=1)
    total = pltpu.roll(
        count[rows : 2 * rows] + count[2 * rows : 3 * rows] + count[3 * rows : 4 * rows], lanes - H, axis=1
    )
    forcing = number * field - total

    centre = field[H : H + cx, 0:cy]
    stacked = jnp.concatenate(list(pieces(centre)) + [jnp.zeros_like(centre)], axis=0)
    turned = stacked.T.astype(jnp.bfloat16)

    def look_up(i):
        base = i * at_once
        xs = row_of(base, 0) - x0
        ys = row_of(base, 1) - y0
        at_x = lax.broadcasted_iota(jnp.int32, (cx, span), 0).astype(jnp.float32) == xs
        at_y = lax.broadcasted_iota(jnp.int32, (cy, span), 0).astype(jnp.float32) == ys
        pick = jnp.where(at_x, 1.0, 0.0).astype(jnp.bfloat16)
        picked = jnp.dot(
            turned, jnp.concatenate([pick] * 4, axis=0), preferred_element_type=jnp.float32
        )
        found = jnp.sum(jnp.where(at_y, picked, 0.0), axis=0, keepdims=True)
        width = snd.shape[2]
        for b in range(at_once):
            for r in range(nrow):
                k = b * nrow + r
                values[base + b, r : r + 1, :] = found[:, k * width : (k + 1) * width]

    loop_over(0, groups // at_once, look_up)

    def back_copy(d):
        return pltpu.make_async_remote_copy(
            src_ref=values.at[lax.rem(me + d, groups)], dst_ref=returned.at[d],
            send_sem=back_send.at[d], recv_sem=back_recv.at[d],
            device_id=group_id(d), device_id_type=MESH,
        )

    loop_over(1, groups, lambda d: back_copy(d).start())

    for l in range(levels):
        adj = forcing
        for step in range(STEPS):
            adj = (
                coef[l, 0] * adj
                + pltpu.roll(coef[l, 2] * adj, rows - 1, axis=0)
                + pltpu.roll(coef[l, 1] * adj, 1, axis=0)
                + pltpu.roll(coef[l, 4] * adj, lanes - 1, axis=1)
                + pltpu.roll(coef[l, 3] * adj, 1, axis=1)
            )
        inner = adj[H : H + cx, 0:cy]
        for t in range(tracers):
            grad_ref[t * levels + l] = weight_ref[t, l] * inner

    loop_over(1, groups, lambda d: back_copy(d).wait_recv())
    model = values[me]
    for d in range(1, groups):
        model = model + returned[d]
    model_ref[...] = model
    loop_over(1, groups, lambda d: back_copy(d).wait_send())


def shards(n_gx, n_gy, initial_conc, diffusivity, wind_east, wind_north, level_weight, owner, column, observed):
    tracers, levels, cx, cy = initial_conc.shape
    fields = tracers * levels
    total = fields + 3 * levels
    groups = n_gx * n_gy
    count = column.shape[0]
    width = min(128, count)
    nrow = count // width
    rows, lanes = cx + 2 * H, 2 * cy
    per = cy // (2 * H)
    packs = -(-total // per)
    f32 = jnp.float32
    vmem = pl.BlockSpec(memory_space=pltpu.VMEM)
    held = pl.BlockSpec(memory_space=pl.ANY)
    dma = pltpu.SemaphoreType.DMA
    conc, model, grad = pl.pallas_call(
        functools.partial(kernel, (n_gx, n_gy, tracers, levels, cx, cy)),
        out_shape=(
            jax.ShapeDtypeStruct((fields, cx, cy), f32),
            jax.ShapeDtypeStruct((nrow, width), f32),
            jax.ShapeDtypeStruct((fields, cx, cy), f32),
        ),
        in_specs=[held] * 4 + [pl.BlockSpec(memory_space=pltpu.SMEM)] + [held] * 3,
        out_specs=(vmem, vmem, vmem),
        scratch_shapes=[
            pltpu.VMEM((total, rows, lanes), f32),
            pltpu.VMEM((fields, rows, lanes), f32),
            pltpu.VMEM((packs, cx, cy), f32),
            pltpu.VMEM((packs, rows, cy), f32),
            pltpu.VMEM((packs, rows, cy), f32),
            pltpu.VMEM((levels, 5, rows, lanes), f32),
            pltpu.VMEM((3 * nrow, width), f32),
            pltpu.VMEM((groups, 3 * nrow, width), f32),
            pltpu.VMEM((4 * rows, lanes), f32),
            pltpu.VMEM((rows, lanes), f32),
            pltpu.VMEM((rows, lanes), f32),
            pltpu.VMEM((groups, nrow, width), f32),
            pltpu.VMEM((groups, nrow, width), f32),
            dma((len(SIDES),)), dma((len(SIDES),)),
            dma((groups,)), dma((groups,)),
            dma, dma,
            dma((groups,)), dma((groups,)),
            pltpu.VMEM((nrow, width), jnp.int32),
            pltpu.VMEM((nrow, width), jnp.int32),
            pltpu.VMEM((nrow, width), f32),
            dma((7,)),
        ],
        compiler_params=pltpu.CompilerParams(
            collective_id=0, has_side_effects=True, vmem_limit_bytes=48 * 1024 * 1024
        ),
        cost_estimate=pl.CostEstimate(flops=2 * 10**9, bytes_accessed=2 * 10**6, transcendentals=0),
    )(
        initial_conc.reshape(fields, cx, cy), diffusivity, wind_east, wind_north, level_weight,
        owner.reshape(nrow, width), column.reshape(nrow, width), observed.reshape(nrow, width),
    )
    shape = (tracers, levels, cx, cy)
    return conc.reshape(shape), model.reshape(count), grad.reshape(shape)


def solution(mesh):
    return jax.shard_map(
        functools.partial(shards, mesh.shape["gx"], mesh.shape["gy"]),
        mesh=mesh,
        in_specs=(
            P(None, "lev", "gx", "gy"),
            P("lev", "gx", "gy"),
            P("lev", "gx", "gy"),
            P("lev", "gx", "gy"),
            P(None, "lev"),
            P(("gx", "gy"), None),
            P(("gx", "gy")),
            P(("gx", "gy")),
        ),
        out_specs=(P(None, "lev", "gx", "gy"), P(("gx", "gy")), P(None, "lev", "gx", "gy")),
        check_vma=False,
    )
```

```python
import functools
import jax
import jax.numpy as jnp
from jax import lax
from jax.experimental import pallas as pl
from jax.experimental.pallas import tpu as pltpu
from jax.sharding import PartitionSpec as P

STEPS = 4
H = 2 * STEPS
MESH = pl.DeviceIdType.MESH
SIDES = [(-1, 0), (1, 0), (0, -1), (0, 1), (-1, -1), (-1, 1), (1, -1), (1, 1)]


def pieces(value):
    high = value.astype(jnp.bfloat16).astype(jnp.float32)
    rest = value - high
    middle = rest.astype(jnp.bfloat16).astype(jnp.float32)
    return high, middle, rest - middle


def kernel(
    sizes,
    conc_ref, diff_ref, east_ref, north_ref, weight_ref, owner_ref, column_ref, observed_ref,
    forecast_ref, model_ref, grad_ref,
    ext, other, pack, from_left, from_right, coef, mine, snd, count, part, arrived, values, returned,
    halo_send, halo_recv, snd_send, snd_recv, part_send, part_recv, back_send, back_recv,
    owner_in, column_in, observed_in, load_sem,
):
    n_gx, n_gy, tracers, levels, cx, cy = sizes
    groups = n_gx * n_gy
    fields = tracers * levels
    rows, lanes = cx + 2 * H, 2 * cy
    lev, gx, gy = lax.axis_index("lev"), lax.axis_index("gx"), lax.axis_index("gy")
    me = gx * n_gy + gy

    def group_id(d):
        target = lax.rem(me + d, groups)
        return (lev, target // n_gy, lax.rem(target, n_gy))

    loads = []
    begin = 0
    for ref in (conc_ref, diff_ref, east_ref, north_ref):
        place = ext.at[pl.ds(begin, ref.shape[0]), pl.ds(H, cx), pl.ds(0, cy)]
        loads.append(pltpu.make_async_copy(ref, place, load_sem.at[len(loads)]))
        begin += ref.shape[0]
    for ref, place in ((owner_ref, owner_in), (column_ref, column_in), (observed_ref, observed_in)):
        loads.append(pltpu.make_async_copy(ref, place, load_sem.at[len(loads)]))
    for load in loads:
        load.start()

    ext[:, 0:H, 0:cy] = jnp.zeros((ext.shape[0], H, cy), jnp.float32)
    ext[:, H + cx : rows, 0:cy] = jnp.zeros((ext.shape[0], H, cy), jnp.float32)
    from_left[...] = jnp.zeros(from_left.shape, jnp.float32)
    from_right[...] = jnp.zeros(from_right.shape, jnp.float32)

    barrier = pltpu.get_barrier_semaphore()

    def greet(d, carry):
        pl.semaphore_signal(barrier, inc=1, device_id=group_id(d), device_id_type=MESH)
        return carry

    lax.fori_loop(1, groups, greet, 0)
    pl.semaphore_signal(barrier, inc=1, device_id=(1 - lev, gx, gy), device_id_type=MESH)

    for load in loads:
        load.wait()

    lane = lax.broadcasted_iota(jnp.int32, (cx, cy), 1)
    per = cy // (2 * H)
    packed = [jnp.zeros((cx, cy), jnp.float32) for _ in range(pack.shape[0])]
    for f in range(ext.shape[0]):
        field = ext[f, H : H + cx, 0:cy]
        g, at = divmod(f, per)
        shift = 2 * H * at
        moved = pltpu.roll(field, shift, axis=1) if shift else field
        slot = lax.rem(lane + H, cy) // (2 * H)
        packed[g] = jnp.where(slot == at, moved, packed[g])
    for g in range(pack.shape[0]):
        pack[g] = packed[g]
    owner, column = owner_in[...], column_in[...]
    nrow = owner.shape[0]
    mine[0:nrow] = ((owner // n_gy) * cx + column // cy).astype(jnp.float32)
    mine[nrow : 2 * nrow] = (lax.rem(owner, n_gy) * cy + lax.rem(column, cy)).astype(jnp.float32)
    mine[2 * nrow : 3 * nrow] = observed_in[...]
    snd[me] = mine[...]

    pl.semaphore_wait(barrier, groups)

    def inside(dx, dy):
        x, y = gx + dx, gy + dy
        return (x >= 0) & (x < n_gx) & (y >= 0) & (y < n_gy)

    def halo_copy(k):
        dx, dy = SIDES[k]
        start, length, to = {-1: (0, H, H + cx), 0: (0, cx, H), 1: (cx - H, H, 0)}[dx]
        if dy == 0:
            src = ext.at[:, pl.ds(H + start, length), pl.ds(0, cy)]
            dst = ext.at[:, pl.ds(to, length), pl.ds(0, cy)]
        else:
            src = pack.at[:, pl.ds(start, length), :]
            dst = (from_right if dy < 0 else from_left).at[:, pl.ds(to, length), :]
        return pltpu.make_async_remote_copy(
            src_ref=src, dst_ref=dst, send_sem=halo_send.at[k], recv_sem=halo_recv.at[k],
            device_id=(lev, gx + dx, gy + dy), device_id_type=MESH,
        )

    for k, (dx, dy) in enumerate(SIDES):
        pl.when(inside(dx, dy))(lambda k=k: halo_copy(k).start())

    def snd_copy(d):
        return pltpu.make_async_remote_copy(
            src_ref=mine, dst_ref=snd.at[me], send_sem=snd_send.at[d], recv_sem=snd_recv.at[d],
            device_id=group_id(d), device_id_type=MESH,
        )

    def loop_over(low, high, body):
        def step(i, carry):
            body(i)
            return carry

        lax.fori_loop(low, high, step, 0)

    loop_over(1, groups, lambda d: snd_copy(d).start())

    for k, (dx, dy) in enumerate(SIDES):
        pl.when(inside(-dx, -dy))(lambda k=k: halo_copy(k).wait_recv())

    wide = lax.broadcasted_iota(jnp.int32, (rows, cy), 1)
    for g in range(pack.shape[0]):
        both = jnp.where(lax.rem(wide, 2 * H) < H, from_right[g], from_left[g])
        for at in range(min(per, ext.shape[0] - g * per)):
            shift = 2 * H * at
            moved = pltpu.roll(both, cy - shift, axis=1) if shift else both
            ext[g * per + at, :, cy:lanes] = jnp.where((wide < H) | (wide >= cy - H), moved, 0.0)
    for l in range(levels):
        kappa = ext[fields + l]
        u = 0.5 * ext[fields + levels + l]
        v = 0.5 * ext[fields + 2 * levels + l]
        coef[l, 0] = 1.0 - 4.0 * kappa
        coef[l, 1] = kappa - u
        coef[l, 2] = kappa + u
        coef[l, 3] = kappa - v
        coef[l, 4] = kappa + v

    def stepped(c, l):
        return (
            coef[l, 0] * c
            + coef[l, 1] * pltpu.roll(c, rows - 1, axis=0)
            + coef[l, 2] * pltpu.roll(c, 1, axis=0)
            + coef[l, 3] * pltpu.roll(c, lanes - 1, axis=1)
            + coef[l, 4] * pltpu.roll(c, 1, axis=1)
        )

    for step in range(STEPS):
        source, target = (ext, other) if step % 2 == 0 else (other, ext)
        if step == 1:
            for k, (dx, dy) in enumerate(SIDES):
                pl.when(inside(dx, dy))(lambda k=k: halo_copy(k).wait_send())
        if step < STEPS - 1:
            def advance(t):
                for l in range(levels):
                    target[t * levels + l] = stepped(source[t * levels + l], l)

            loop_over(0, tracers, advance)
        else:
            part[...] = jnp.zeros(part.shape, jnp.float32)

            def finish(t):
                total = part[...]
                for l in range(levels):
                    result = stepped(source[t * levels + l], l)
                    forecast_ref[t * levels + l] = result[H : H + cx, 0:cy]
                    total = total + weight_ref[t, l] * result
                part[...] = total

            loop_over(0, tracers, finish)

    part_copy = pltpu.make_async_remote_copy(
        src_ref=part, dst_ref=arrived, send_sem=part_send, recv_sem=part_recv,
        device_id=(1 - lev, gx, gy), device_id_type=MESH,
    )
    part_copy.start()

    loop_over(1, groups, lambda d: snd_copy(d).wait_recv())
    loop_over(1, groups, lambda d: snd_copy(d).wait_send())
    at_once = 4
    x0 = (gx * cx).astype(jnp.float32)
    y0 = (gy * cy).astype(jnp.float32)

    def row_of(base, kind):
        return jnp.concatenate(
            [snd[base + b, kind * nrow + r : kind * nrow + r + 1, :] for b in range(at_once) for r in range(nrow)],
            axis=1,
        )

    span = at_once * nrow * snd.shape[2]
    compact = cy + 2 * H
    count[...] = jnp.zeros(count.shape, jnp.float32)

    def tally(i):
        base = i * at_once
        xs = row_of(base, 0) - (x0 - H)
        ys = row_of(base, 1) - (y0 - H)
        obs = row_of(base, 2)
        at_x = lax.broadcasted_iota(jnp.int32, (rows, span), 0).astype(jnp.float32) == xs
        at_y = lax.broadcasted_iota(jnp.int32, (compact, span), 0).astype(jnp.float32) == ys
        stack = [jnp.where(at_x, 1.0, 0.0)] + [jnp.where(at_x, piece, 0.0) for piece in pieces(obs)]
        left = jnp.concatenate([s.astype(jnp.bfloat16) for s in stack], axis=0)
        right = jnp.where(at_y, 1.0, 0.0).astype(jnp.bfloat16)
        count[:, 0:compact] += lax.dot_general(
            left, right, (((1,), (1,)), ((), ())), preferred_element_type=jnp.float32
        )

    loop_over(0, groups // at_once, tally)

    part_copy.wait()
    field = part[...] + arrived[...]
    number = pltpu.roll(count[0:rows], lanes - H, axis=1)
    total = pltpu.roll(
        count[rows : 2 * rows] + count[2 * rows : 3 * rows] + count[3 * rows : 4 * rows], lanes - H, axis=1
    )
    forcing = number * field - total

    centre = field[H : H + cx, 0:cy]
    stacked = jnp.concatenate(list(pieces(centre)) + [jnp.zeros_like(centre)], axis=0)
    turned = stacked.T.astype(jnp.bfloat16)

    def look_up(i):
        base = i * at_once
        xs = row_of(base, 0) - x0
        ys = row_of(base, 1) - y0
        at_x = lax.broadcasted_iota(jnp.int32, (cx, span), 0).astype(jnp.float32) == xs
        at_y = lax.broadcasted_iota(jnp.int32, (cy, span), 0).astype(jnp.float32) == ys
        pick = jnp.where(at_x, 1.0, 0.0).astype(jnp.bfloat16)
        picked = jnp.dot(
            turned, jnp.concatenate([pick] * 4, axis=0), preferred_element_type=jnp.float32
        )
        found = jnp.sum(jnp.where(at_y, picked, 0.0), axis=0, keepdims=True)
        width = snd.shape[2]
        for b in range(at_once):
            for r in range(nrow):
                k = b * nrow + r
                values[base + b, r : r + 1, :] = found[:, k * width : (k + 1) * width]

    loop_over(0, groups // at_once, look_up)

    def back_copy(d):
        return pltpu.make_async_remote_copy(
            src_ref=values.at[lax.rem(me + d, groups)], dst_ref=returned.at[d],
            send_sem=back_send.at[d], recv_sem=back_recv.at[d],
            device_id=group_id(d), device_id_type=MESH,
        )

    loop_over(1, groups, lambda d: back_copy(d).start())

    for l in range(levels):
        adj = forcing
        for step in range(STEPS):
            adj = (
                coef[l, 0] * adj
                + pltpu.roll(coef[l, 2] * adj, rows - 1, axis=0)
                + pltpu.roll(coef[l, 1] * adj, 1, axis=0)
                + pltpu.roll(coef[l, 4] * adj, lanes - 1, axis=1)
                + pltpu.roll(coef[l, 3] * adj, 1, axis=1)
            )
        inner = adj[H : H + cx, 0:cy]
        for t in range(tracers):
            grad_ref[t * levels + l] = weight_ref[t, l] * inner

    loop_over(1, groups, lambda d: back_copy(d).wait_recv())
    model = values[me]
    for d in range(1, groups):
        model = model + returned[d]
    model_ref[...] = model
    loop_over(1, groups, lambda d: back_copy(d).wait_send())


def shards(n_gx, n_gy, initial_conc, diffusivity, wind_east, wind_north, level_weight, owner, column, observed):
    tracers, levels, cx, cy = initial_conc.shape
    fields = tracers * levels
    total = fields + 3 * levels
    groups = n_gx * n_gy
    count = column.shape[0]
    width = min(128, count)
    nrow = count // width
    rows, lanes = cx + 2 * H, 2 * cy
    per = cy // (2 * H)
    packs = -(-total // per)
    f32 = jnp.float32
    vmem = pl.BlockSpec(memory_space=pltpu.VMEM)
    held = pl.BlockSpec(memory_space=pltpu.HBM)
    dma = pltpu.SemaphoreType.DMA
    conc, model, grad = pl.pallas_call(
        functools.partial(kernel, (n_gx, n_gy, tracers, levels, cx, cy)),
        out_shape=(
            jax.ShapeDtypeStruct((fields, cx, cy), f32),
            jax.ShapeDtypeStruct((nrow, width), f32),
            jax.ShapeDtypeStruct((fields, cx, cy), f32),
        ),
        in_specs=[held] * 4 + [pl.BlockSpec(memory_space=pltpu.SMEM)] + [held] * 3,
        out_specs=(vmem, vmem, vmem),
        scratch_shapes=[
            pltpu.VMEM((total, rows, lanes), f32),
            pltpu.VMEM((fields, rows, lanes), f32),
            pltpu.VMEM((packs, cx, cy), f32),
            pltpu.VMEM((packs, rows, cy), f32),
            pltpu.VMEM((packs, rows, cy), f32),
            pltpu.VMEM((levels, 5, rows, lanes), f32),
            pltpu.VMEM((3 * nrow, width), f32),
            pltpu.VMEM((groups, 3 * nrow, width), f32),
            pltpu.VMEM((4 * rows, lanes), f32),
            pltpu.VMEM((rows, lanes), f32),
            pltpu.VMEM((rows, lanes), f32),
            pltpu.VMEM((groups, nrow, width), f32),
            pltpu.VMEM((groups, nrow, width), f32),
            dma((len(SIDES),)), dma((len(SIDES),)),
            dma((groups,)), dma((groups,)),
            dma, dma,
            dma((groups,)), dma((groups,)),
            pltpu.VMEM((nrow, width), jnp.int32),
            pltpu.VMEM((nrow, width), jnp.int32),
            pltpu.VMEM((nrow, width), f32),
            dma((7,)),
        ],
        compiler_params=pltpu.CompilerParams(
            collective_id=0, has_side_effects=True, vmem_limit_bytes=48 * 1024 * 1024
        ),
        cost_estimate=pl.CostEstimate(flops=2 * 10**9, bytes_accessed=2 * 10**6, transcendentals=0),
    )(
        initial_conc.reshape(fields, cx, cy), diffusivity, wind_east, wind_north, level_weight,
        owner.reshape(nrow, width), column.reshape(nrow, width), observed.reshape(nrow, width),
    )
    shape = (tracers, levels, cx, cy)
    return conc.reshape(shape), model.reshape(count), grad.reshape(shape)


def solution(mesh):
    return jax.shard_map(
        functools.partial(shards, mesh.shape["gx"], mesh.shape["gy"]),
        mesh=mesh,
        in_specs=(
            P(None, "lev", "gx", "gy"),
            P("lev", "gx", "gy"),
            P("lev", "gx", "gy"),
            P("lev", "gx", "gy"),
            P(None, "lev"),
            P(("gx", "gy"), None),
            P(("gx", "gy")),
            P(("gx", "gy")),
        ),
        out_specs=(P(None, "lev", "gx", "gy"), P(("gx", "gy")), P(None, "lev", "gx", "gy")),
        check_vma=False,
    )
```

```python
import functools
import jax
import jax.numpy as jnp
from jax import lax
from jax.experimental import pallas as pl
from jax.experimental.pallas import tpu as pltpu
from jax.sharding import PartitionSpec as P

STEPS = 4
H = 2 * STEPS
MESH = pl.DeviceIdType.MESH
SIDES = [(-1, 0), (1, 0), (0, -1), (0, 1), (-1, -1), (-1, 1), (1, -1), (1, 1)]


def pieces(value):
    high = value.astype(jnp.bfloat16).astype(jnp.float32)
    rest = value - high
    middle = rest.astype(jnp.bfloat16).astype(jnp.float32)
    return high, middle, rest - middle


def kernel(
    sizes,
    conc_ref, diff_ref, east_ref, north_ref, weight_ref, owner_ref, column_ref, observed_ref,
    forecast_ref, model_ref, grad_ref,
    ext, other, pack, from_left, from_right, coef, mine, snd, count, part, arrived, values, returned,
    halo_send, halo_recv, snd_send, snd_recv, part_send, part_recv, back_send, back_recv,
):
    n_gx, n_gy, tracers, levels, cx, cy = sizes
    groups = n_gx * n_gy
    fields = tracers * levels
    rows, lanes = cx + 2 * H, 2 * cy
    lev, gx, gy = lax.axis_index("lev"), lax.axis_index("gx"), lax.axis_index("gy")
    me = gx * n_gy + gy

    def group_id(d):
        target = lax.rem(me + d, groups)
        return (lev, target // n_gy, lax.rem(target, n_gy))

    ext[:, 0:H, 0:cy] = jnp.zeros((ext.shape[0], H, cy), jnp.float32)
    ext[:, H + cx : rows, 0:cy] = jnp.zeros((ext.shape[0], H, cy), jnp.float32)
    from_left[...] = jnp.zeros(from_left.shape, jnp.float32)
    from_right[...] = jnp.zeros(from_right.shape, jnp.float32)

    barrier = pltpu.get_barrier_semaphore()

    def greet(d, carry):
        pl.semaphore_signal(barrier, inc=1, device_id=group_id(d), device_id_type=MESH)
        return carry

    lax.fori_loop(1, groups, greet, 0)
    pl.semaphore_signal(barrier, inc=1, device_id=(1 - lev, gx, gy), device_id_type=MESH)

    lane = lax.broadcasted_iota(jnp.int32, (cx, cy), 1)
    per = cy // (2 * H)
    packed = [jnp.zeros((cx, cy), jnp.float32) for _ in range(pack.shape[0])]
    for f in range(ext.shape[0]):
        if f < fields:
            field = conc_ref[f]
        else:
            which, l = divmod(f - fields, levels)
            field = (diff_ref, east_ref, north_ref)[which][l]
        ext[f, H : H + cx, 0:cy] = field
        g, at = divmod(f, per)
        shift = 2 * H * at
        moved = pltpu.roll(field, shift, axis=1) if shift else field
        slot = lax.rem(lane + H, cy) // (2 * H)
        packed[g] = jnp.where(slot == at, moved, packed[g])
    for g in range(pack.shape[0]):
        pack[g] = packed[g]
    owner, column = owner_ref[...], column_ref[...]
    nrow = owner.shape[0]
    mine[0:nrow] = ((owner // n_gy) * cx + column // cy).astype(jnp.float32)
    mine[nrow : 2 * nrow] = (lax.rem(owner, n_gy) * cy + lax.rem(column, cy)).astype(jnp.float32)
    mine[2 * nrow : 3 * nrow] = observed_ref[...]
    snd[me] = mine[...]

    pl.semaphore_wait(barrier, groups)

    def inside(dx, dy):
        x, y = gx + dx, gy + dy
        return (x >= 0) & (x < n_gx) & (y >= 0) & (y < n_gy)

    def halo_copy(k):
        dx, dy = SIDES[k]
        start, length, to = {-1: (0, H, H + cx), 0: (0, cx, H), 1: (cx - H, H, 0)}[dx]
        if dy == 0:
            src = ext.at[:, pl.ds(H + start, length), pl.ds(0, cy)]
            dst = ext.at[:, pl.ds(to, length), pl.ds(0, cy)]
        else:
            src = pack.at[:, pl.ds(start, length), :]
            dst = (from_right if dy < 0 else from_left).at[:, pl.ds(to, length), :]
        return pltpu.make_async_remote_copy(
            src_ref=src, dst_ref=dst, send_sem=halo_send.at[k], recv_sem=halo_recv.at[k],
            device_id=(lev, gx + dx, gy + dy), device_id_type=MESH,
        )

    for k, (dx, dy) in enumerate(SIDES):
        pl.when(inside(dx, dy))(lambda k=k: halo_copy(k).start())

    def snd_copy(d):
        return pltpu.make_async_remote_copy(
            src_ref=mine, dst_ref=snd.at[me], send_sem=snd_send.at[d], recv_sem=snd_recv.at[d],
            device_id=group_id(d), device_id_type=MESH,
        )

    def loop_over(low, high, body):
        def step(i, carry):
            body(i)
            return carry

        lax.fori_loop(low, high, step, 0)

    loop_over(1, groups, lambda d: snd_copy(d).start())

    for k, (dx, dy) in enumerate(SIDES):
        pl.when(inside(-dx, -dy))(lambda k=k: halo_copy(k).wait_recv())

    wide = lax.broadcasted_iota(jnp.int32, (rows, cy), 1)
    for g in range(pack.shape[0]):
        both = jnp.where(lax.rem(wide, 2 * H) < H, from_right[g], from_left[g])
        for at in range(min(per, ext.shape[0] - g * per)):
            shift = 2 * H * at
            moved = pltpu.roll(both, cy - shift, axis=1) if shift else both
            ext[g * per + at, :, cy:lanes] = jnp.where((wide < H) | (wide >= cy - H), moved, 0.0)
    for l in range(levels):
        kappa = ext[fields + l]
        u = 0.5 * ext[fields + levels + l]
        v = 0.5 * ext[fields + 2 * levels + l]
        coef[l, 0] = 1.0 - 4.0 * kappa
        coef[l, 1] = kappa - u
        coef[l, 2] = kappa + u
        coef[l, 3] = kappa - v
        coef[l, 4] = kappa + v

    def stepped(c, l):
        return (
            coef[l, 0] * c
            + coef[l, 1] * pltpu.roll(c, rows - 1, axis=0)
            + coef[l, 2] * pltpu.roll(c, 1, axis=0)
            + coef[l, 3] * pltpu.roll(c, lanes - 1, axis=1)
            + coef[l, 4] * pltpu.roll(c, 1, axis=1)
        )

    for step in range(STEPS):
        source, target = (ext, other) if step % 2 == 0 else (other, ext)
        if step == 1:
            for k, (dx, dy) in enumerate(SIDES):
                pl.when(inside(dx, dy))(lambda k=k: halo_copy(k).wait_send())
        if step < STEPS - 1:
            def advance(t):
                for l in range(levels):
                    target[t * levels + l] = stepped(source[t * levels + l], l)

            lax.fori_loop(0, tracers, lambda t, c: (advance(t), c)[1], 0, unroll=True)
        else:
            part[...] = jnp.zeros(part.shape, jnp.float32)

            def finish(t):
                total = part[...]
                for l in range(levels):
                    result = stepped(source[t * levels + l], l)
                    forecast_ref[t * levels + l] = result[H : H + cx, 0:cy]
                    total = total + weight_ref[t, l] * result
                part[...] = total

            lax.fori_loop(0, tracers, lambda t, c: (finish(t), c)[1], 0, unroll=True)

    part_copy = pltpu.make_async_remote_copy(
        src_ref=part, dst_ref=arrived, send_sem=part_send, recv_sem=part_recv,
        device_id=(1 - lev, gx, gy), device_id_type=MESH,
    )
    part_copy.start()

    loop_over(1, groups, lambda d: snd_copy(d).wait_recv())
    loop_over(1, groups, lambda d: snd_copy(d).wait_send())
    at_once = 4
    x0 = (gx * cx).astype(jnp.float32)
    y0 = (gy * cy).astype(jnp.float32)

    def row_of(base, kind):
        return jnp.concatenate(
            [snd[base + b, kind * nrow + r : kind * nrow + r + 1, :] for b in range(at_once) for r in range(nrow)],
            axis=1,
        )

    span = at_once * nrow * snd.shape[2]
    compact = cy + 2 * H
    count[...] = jnp.zeros(count.shape, jnp.float32)

    def tally(i):
        base = i * at_once
        xs = row_of(base, 0) - (x0 - H)
        ys = row_of(base, 1) - (y0 - H)
        obs = row_of(base, 2)
        at_x = lax.broadcasted_iota(jnp.int32, (rows, span), 0).astype(jnp.float32) == xs
        at_y = lax.broadcasted_iota(jnp.int32, (compact, span), 0).astype(jnp.float32) == ys
        stack = [jnp.where(at_x, 1.0, 0.0)] + [jnp.where(at_x, piece, 0.0) for piece in pieces(obs)]
        left = jnp.concatenate([s.astype(jnp.bfloat16) for s in stack], axis=0)
        right = jnp.where(at_y, 1.0, 0.0).astype(jnp.bfloat16)
        count[:, 0:compact] += lax.dot_general(
            left, right, (((1,), (1,)), ((), ())), preferred_element_type=jnp.float32
        )

    loop_over(0, groups // at_once, tally)

    part_copy.wait()
    field = part[...] + arrived[...]
    number = pltpu.roll(count[0:rows], lanes - H, axis=1)
    total = pltpu.roll(
        count[rows : 2 * rows] + count[2 * rows : 3 * rows] + count[3 * rows : 4 * rows], lanes - H, axis=1
    )
    forcing = number * field - total

    centre = field[H : H + cx, 0:cy]
    stacked = jnp.concatenate(list(pieces(centre)) + [jnp.zeros_like(centre)], axis=0)
    turned = stacked.T.astype(jnp.bfloat16)

    def look_up(i):
        base = i * at_once
        xs = row_of(base, 0) - x0
        ys = row_of(base, 1) - y0
        at_x = lax.broadcasted_iota(jnp.int32, (cx, span), 0).astype(jnp.float32) == xs
        at_y = lax.broadcasted_iota(jnp.int32, (cy, span), 0).astype(jnp.float32) == ys
        pick = jnp.where(at_x, 1.0, 0.0).astype(jnp.bfloat16)
        picked = jnp.dot(
            turned, jnp.concatenate([pick] * 4, axis=0), preferred_element_type=jnp.float32
        )
        found = jnp.sum(jnp.where(at_y, picked, 0.0), axis=0, keepdims=True)
        width = snd.shape[2]
        for b in range(at_once):
            for r in range(nrow):
                k = b * nrow + r
                values[base + b, r : r + 1, :] = found[:, k * width : (k + 1) * width]

    loop_over(0, groups // at_once, look_up)

    def back_copy(d):
        return pltpu.make_async_remote_copy(
            src_ref=values.at[lax.rem(me + d, groups)], dst_ref=returned.at[d],
            send_sem=back_send.at[d], recv_sem=back_recv.at[d],
            device_id=group_id(d), device_id_type=MESH,
        )

    loop_over(1, groups, lambda d: back_copy(d).start())

    for l in range(levels):
        adj = forcing
        for step in range(STEPS):
            adj = (
                coef[l, 0] * adj
                + pltpu.roll(coef[l, 2] * adj, rows - 1, axis=0)
                + pltpu.roll(coef[l, 1] * adj, 1, axis=0)
                + pltpu.roll(coef[l, 4] * adj, lanes - 1, axis=1)
                + pltpu.roll(coef[l, 3] * adj, 1, axis=1)
            )
        inner = adj[H : H + cx, 0:cy]
        for t in range(tracers):
            grad_ref[t * levels + l] = weight_ref[t, l] * inner

    loop_over(1, groups, lambda d: back_copy(d).wait_recv())
    model = values[me]
    for d in range(1, groups):
        model = model + returned[d]
    model_ref[...] = model
    loop_over(1, groups, lambda d: back_copy(d).wait_send())


def shards(n_gx, n_gy, initial_conc, diffusivity, wind_east, wind_north, level_weight, owner, column, observed):
    tracers, levels, cx, cy = initial_conc.shape
    fields = tracers * levels
    total = fields + 3 * levels
    groups = n_gx * n_gy
    count = column.shape[0]
    width = min(128, count)
    nrow = count // width
    rows, lanes = cx + 2 * H, 2 * cy
    per = cy // (2 * H)
    packs = -(-total // per)
    f32 = jnp.float32
    vmem = pl.BlockSpec(memory_space=pltpu.VMEM)
    dma = pltpu.SemaphoreType.DMA
    conc, model, grad = pl.pallas_call(
        functools.partial(kernel, (n_gx, n_gy, tracers, levels, cx, cy)),
        out_shape=(
            jax.ShapeDtypeStruct((fields, cx, cy), f32),
            jax.ShapeDtypeStruct((nrow, width), f32),
            jax.ShapeDtypeStruct((fields, cx, cy), f32),
        ),
        in_specs=[vmem] * 4 + [pl.BlockSpec(memory_space=pltpu.SMEM)] + [vmem] * 3,
        out_specs=(vmem, vmem, vmem),
        scratch_shapes=[
            pltpu.VMEM((total, rows, lanes), f32),
            pltpu.VMEM((fields, rows, lanes), f32),
            pltpu.VMEM((packs, cx, cy), f32),
            pltpu.VMEM((packs, rows, cy), f32),
            pltpu.VMEM((packs, rows, cy), f32),
            pltpu.VMEM((levels, 5, rows, lanes), f32),
            pltpu.VMEM((3 * nrow, width), f32),
            pltpu.VMEM((groups, 3 * nrow, width), f32),
            pltpu.VMEM((4 * rows, lanes), f32),
            pltpu.VMEM((rows, lanes), f32),
            pltpu.VMEM((rows, lanes), f32),
            pltpu.VMEM((groups, nrow, width), f32),
            pltpu.VMEM((groups, nrow, width), f32),
            dma((len(SIDES),)), dma((len(SIDES),)),
            dma((groups,)), dma((groups,)),
            dma, dma,
            dma((groups,)), dma((groups,)),
        ],
        compiler_params=pltpu.CompilerParams(
            collective_id=0, has_side_effects=True, vmem_limit_bytes=48 * 1024 * 1024
        ),
        cost_estimate=pl.CostEstimate(flops=2 * 10**9, bytes_accessed=2 * 10**6, transcendentals=0),
    )(
        initial_conc.reshape(fields, cx, cy), diffusivity, wind_east, wind_north, level_weight,
        owner.reshape(nrow, width), column.reshape(nrow, width), observed.reshape(nrow, width),
    )
    shape = (tracers, levels, cx, cy)
    return conc.reshape(shape), model.reshape(count), grad.reshape(shape)


def solution(mesh):
    return jax.shard_map(
        functools.partial(shards, mesh.shape["gx"], mesh.shape["gy"]),
        mesh=mesh,
        in_specs=(
            P(None, "lev", "gx", "gy"),
            P("lev", "gx", "gy"),
            P("lev", "gx", "gy"),
            P("lev", "gx", "gy"),
            P(None, "lev"),
            P(("gx", "gy"), None),
            P(("gx", "gy")),
            P(("gx", "gy")),
        ),
        out_specs=(P(None, "lev", "gx", "gy"), P(("gx", "gy")), P(None, "lev", "gx", "gy")),
        check_vma=False,
    )
```
